32 devices in a mesh: sub: 16 (over z, y, core), grp: 2 (over x).
Axes of the slice: x: 2, y: 2, z: 4, core: 2. Of those that a mesh axis runs over, the one named last changes fastest.
Arguments:
- margin_basis: bfloat16 [32, 6, 384, 128], P(('sub', 'grp')), may hold values from -6 to 6
- pair_matrix: bfloat16 [32, 6, 384, 384], P(('sub', 'grp')), as said below
- own_basis: bfloat16 [32, 2048, 128], P(('sub', 'grp')), may hold values from -0.125 to 0.125
- own_image: bfloat16 [32, 2048, 128], P(('sub', 'grp')), may hold values from -6 to 6
- tile_counts: int32 [32, 6], P(('sub', 'grp')), may hold values from 0 to 3, as said below
Outputs:
- coarse_rows: float32 [32, 7, 128, 128], P('sub', None, 'grp')
The draws below stay inside these ranges and needn't reach their ends.
Inputs may be any that keep to these rules, and one draw needn't show every extreme that they name: `tile_counts`: tile counts of the two slots of one neighbour pair are equal, zero for slots without neighbour, and the pairs of subdomains 0 and 1 and of subdomains (7) * 2 and (8) * 2 have 3 tiles in every draw. pair_matrix[s + stride, 2j + 1] is the transpose of pair_matrix[s, 2j] wherever both are neighbours.
All inputs are finite; a program needn't handle non-finite values.
Results may differ from the reference program's by a relative error of at most 0.0026.
Values may be sent and summed in bfloat16 or wider, within the bound.
A program may use at most 64 MiB of HBM per device.

```python
import jax
import jax.numpy as jnp

EIG = 128
ROW_TILE = 128
PAIR_TILES = 3
SPAN = 8
OWN_ROWS = 2048
GROUP = 2
LINES = 16
SUBS = 32
PAIR_ROWS = 384


def draw_tile_counts(key, part):
    index = jnp.arange(SUBS, dtype=jnp.int32)
    coord_x = index % GROUP
    plane = index // GROUP
    upper_tiles = jax.random.randint(jax.random.fold_in(key, 11), (SUBS, 3), 0, PAIR_TILES + 1)
    upper_tiles = upper_tiles.at[0, 0].set(PAIR_TILES)
    upper_tiles = upper_tiles.at[(LINES // 2 - 1) * GROUP, 1].set(PAIR_TILES)
    inside = (coord_x + 1 < GROUP, plane + 1 < LINES, plane + SPAN < LINES)
    below = (coord_x >= 1, plane >= 1, plane >= SPAN)
    columns = []
    for which, stride in enumerate((1, GROUP, SPAN * GROUP)):
        upper = jnp.where(inside[which], upper_tiles[:, which], 0)
        lower = jnp.where(below[which], jnp.roll(upper, stride), 0)
        columns.append(upper)
        columns.append(lower)
    return jnp.stack(columns, axis=1).astype(jnp.int32)


def draw_pair_matrix(key, part):
    shape = (SUBS, 3, PAIR_ROWS, PAIR_ROWS)
    base = jax.random.normal(jax.random.fold_in(key, 21), shape)
    base = (base / PAIR_ROWS).astype(jnp.bfloat16)
    blocks = []
    for which, stride in enumerate((1, GROUP, SPAN * GROUP)):
        upper = base[:, which]
        blocks.append(upper)
        blocks.append(jnp.swapaxes(jnp.roll(upper, stride, axis=0), 1, 2))
    return jnp.stack(blocks, axis=1)


def levels(stream_key, shape, pieces, smallest, high):
    def one(position, blocks):
        heights = jax.random.uniform(jax.random.fold_in(jax.random.fold_in(stream_key, 6), position), (blocks,), jnp.float32, smallest / len(pieces), high / len(pieces))
        return jnp.repeat(jnp.exp(heights), shape[position] // blocks).reshape((-1,) + (1,) * (len(shape) - position - 1))

    gain = one(*pieces[0])
    for cut in pieces[1:]:
        gain = gain * one(*cut)
    return gain


def normal_values(key, shape, spread, most, split=(), held_as=jnp.bfloat16):
    values = spread * jax.random.normal(key, shape, jnp.float32)
    if split:
        values = values * levels(key, shape, split, -0.22, 0.18)
    return jnp.clip(values, -most, most).astype(held_as)


def setup_inputs(seed: int = 0) -> dict:
    key_list = jax.random.split(jax.random.key(seed), 6)
    margin_basis = normal_values(key_list[0], (SUBS, 6, PAIR_ROWS, EIG), 1.0, 6.0, ((0, 32),))
    pair_matrix = draw_pair_matrix(jax.random.fold_in(key_list[5], 71), 0)
    own_basis = normal_values(key_list[2], (SUBS, OWN_ROWS, EIG), OWN_ROWS ** -0.5, 0.125, ((0, 32),))
    own_image = normal_values(key_list[3], (SUBS, OWN_ROWS, EIG), 1.0, 6.0, ((0, 32),))
    tile_counts = draw_tile_counts(jax.random.fold_in(key_list[5], 71), 0)
    return dict(margin_basis=margin_basis, pair_matrix=pair_matrix, own_basis=own_basis, own_image=own_image, tile_counts=tile_counts)


def reference(margin_basis, pair_matrix, own_basis, own_image, tile_counts):
    single = jnp.float32
    diagonal_block = jnp.einsum('sre,srf->sef', own_basis.astype(single), own_image.astype(single))
    row_index = jnp.arange(PAIR_ROWS, dtype=jnp.int32)
    live_rows = row_index[None, None, :, None] < tile_counts[:, :, None, None] * ROW_TILE
    masked_basis = jnp.where(live_rows, margin_basis, jnp.zeros((), jnp.bfloat16))
    blocks = [diagonal_block, None, None, None, None, None, None]
    for which, stride in enumerate((1, GROUP, SPAN * GROUP)):
        upper = 2 * which
        lower = upper + 1
        partner = jnp.roll(masked_basis[:, lower], -stride, axis=0)
        applied = jnp.einsum('src,sce->sre', pair_matrix[:, upper].astype(single), partner.astype(single)).astype(jnp.bfloat16)
        coupling = jnp.einsum('sre,srf->sef', masked_basis[:, upper].astype(single), applied.astype(single))
        blocks[1 + upper] = coupling
        blocks[1 + lower] = jnp.roll(jnp.swapaxes(coupling, 1, 2), stride, axis=0)
    return jnp.stack(blocks, axis=1)
```

```python
import functools

import jax
import jax.numpy as jnp
from jax import lax
from jax.experimental import pallas as pl
from jax.experimental.pallas import tpu as pltpu
from jax.sharding import PartitionSpec as P

ROW_TILE = 128
SPAN = 8
MESH = pl.DeviceIdType.MESH
F32 = jnp.float32
BF16 = jnp.bfloat16


def contract_rows(left, right):
    return lax.dot_general(left, right, (((0,), (0,)), ((), ())), preferred_element_type=F32)


def masked(block, tile_count):
    row_index = lax.broadcasted_iota(jnp.int32, block.shape, 0)
    return jnp.where(row_index < tile_count * ROW_TILE, block, jnp.zeros((), block.dtype))


def kernel(
    lines, group,
    counts, margin, matrix, own_basis, own_image, out,
    m_own, m_got, mats, basis, image, applied, stage,
    load_sem, margin_send, margin_recv, block_send, block_recv,
):
    q = lax.axis_index("sub")
    g = lax.axis_index("grp")
    odd = lax.rem(q, 2) == 1

    directions = (
        (odd, g >= 1, g + 1 < group, (0, 1)),
        (True, q >= 1, q + 1 < lines, (1, 0)),
        (odd, q >= SPAN, q + SPAN < lines, (SPAN, 0)),
    )

    def cases(j):
        up, low, high, _ = directions[j]
        if up is True:
            return ((True, low, high),)
        return (
            (True, jnp.logical_and(up, low), jnp.logical_and(up, high)),
            (False, jnp.logical_and(jnp.logical_not(up), high), jnp.logical_and(jnp.logical_not(up), low)),
        )

    def other(d):
        return lax.rem(g + d, group)

    barrier = pltpu.get_barrier_semaphore()
    for d in range(1, group):
        pl.semaphore_signal(barrier, inc=1, device_id=(q, other(d)), device_id_type=MESH)
    greeted = jnp.int32(group - 1)
    for j in (1, 2):
        _, low, high, (step, _) = directions[j]
        for there, line in ((low, q - step), (high, q + step)):
            @pl.when(there)
            def _():
                for d in range(group):
                    pl.semaphore_signal(barrier, inc=1, device_id=(line, other(d)), device_id_type=MESH)
            greeted = greeted + jnp.where(there, group, 0)

    load_basis = pltpu.make_async_copy(own_basis.at[0], basis, load_sem.at[6])
    load_image = pltpu.make_async_copy(own_image.at[0], image, load_sem.at[7])

    def loads(j, up):
        slot = 2 * j + (1 if up else 0)
        return (
            pltpu.make_async_copy(margin.at[0, slot], m_own.at[j], load_sem.at[2 * j]),
            pltpu.make_async_copy(matrix.at[0, slot], mats.at[j], load_sem.at[2 * j + 1]),
        )

    load_basis.start()
    load_image.start()
    for j in (1, 0, 2):
        for up, computes, _ in cases(j):
            @pl.when(computes)
            def _():
                for copy in loads(j, up):
                    copy.start()

    def margin_copy(j, up):
        sq, sg = directions[j][3]
        target = (q + sq, g + sg) if up else (q - sq, g - sg)
        slot = 2 * j + (0 if up else 1)
        return pltpu.make_async_remote_copy(
            src_ref=margin.at[0, slot], dst_ref=m_got.at[j],
            send_sem=margin_send.at[j], recv_sem=margin_recv.at[j],
            device_id=target, device_id_type=MESH,
        )

    pl.semaphore_wait(barrier, greeted)
    for j in (2, 1, 0):
        for up, _, sends in cases(j):
            @pl.when(sends)
            def _():
                margin_copy(j, up).start()

    def block_copies(block, line, own_line, place, slot):
        return [
            pltpu.make_async_remote_copy(
                src_ref=stage.at[block, other(d)], dst_ref=out.at[place, slot],
                send_sem=block_send.at[block, d], recv_sem=block_recv.at[place, slot],
                device_id=(line, other(d)), device_id_type=MESH,
            )
            for d in range(1 if own_line else 0, group)
        ]

    def deliver(block, value, line, own_line, place, slot):
        stage[block] = value.astype(BF16).reshape(stage.shape[1:])
        for copy in block_copies(block, line, own_line, place, slot):
            copy.start()
        if own_line:
            out[place, slot] = stage[block, g]

    def pair_targets(j, up):
        sq, sg = directions[j][3]
        lower = (q - sq, g - sg) if up else (q, g)
        upper = (q, g) if up else (q + sq, g + sg)
        own_lower = sq == 0 or not up
        own_upper = sq == 0 or up
        return (
            (1 + 2 * j, lower[0], own_lower, lower[1], 1 + 2 * j),
            (2 + 2 * j, upper[0], own_upper, upper[1], 2 + 2 * j),
        )

    load_basis.wait()
    load_image.wait()
    deliver(0, contract_rows(basis[...], image[...]), q, True, g, 0)

    nothing = jnp.zeros(out.shape[2:], BF16)
    out[group - 1, 1] = nothing
    out[0, 2] = nothing
    for j in (1, 2):
        _, low, high, _ = directions[j]
        for there, slot in ((high, 1 + 2 * j), (low, 2 + 2 * j)):
            @pl.when(jnp.logical_not(there))
            def _():
                for place in range(group):
                    out[place, slot] = nothing

    for j in (1, 0, 2):
        for up, computes, _ in cases(j):
            @pl.when(computes)
            def _():
                for copy in loads(j, up):
                    copy.wait()
                if up:
                    count = counts[0, 2 * j + 1]
                    product = contract_rows(mats[j], masked(m_own[j], count))
                    applied[j] = masked(product, count).astype(BF16)

    for j in (1, 0, 2):
        for up, computes, _ in cases(j):
            @pl.when(computes)
            def _():
                margin_copy(j, up).wait_recv()
                if up:
                    coupling = contract_rows(m_got[j], applied[j])
                else:
                    count = counts[0, 2 * j]
                    product = jnp.dot(mats[j], masked(m_got[j], count), preferred_element_type=F32)
                    coupling = contract_rows(m_own[j], masked(product, count).astype(BF16))
                first, second = pair_targets(j, up)
                deliver(first[0], coupling, *first[1:])
                deliver(second[0], coupling.T, *second[1:])

    def arrived(place, slot):
        pltpu.make_async_remote_copy(
            src_ref=stage.at[0, 0], dst_ref=out.at[place, slot],
            send_sem=block_send.at[0, 0], recv_sem=block_recv.at[place, slot],
            device_id=(q, other(1)), device_id_type=MESH,
        ).wait_recv()

    for d in range(1, group):
        arrived(other(d), 0)
    for place in range(group - 1):
        @pl.when(jnp.where(odd, place + 1, place) != g)
        def _():
            arrived(place, 1)
            arrived(place + 1, 2)
    for j in (1, 2):
        up, low, high, _ = directions[j]
        for at_upper in (True, False):
            if up is True:
                if not at_upper:
                    continue
                high_here, low_here = high, low
            else:
                chosen = up if at_upper else jnp.logical_not(up)
                high_here, low_here = jnp.logical_and(chosen, high), jnp.logical_and(chosen, low)

            @pl.when(high_here)
            def _():
                for d in range(0 if at_upper else 1, group):
                    arrived(other(d), 1 + 2 * j)

            @pl.when(low_here)
            def _():
                for d in range(1 if at_upper else 0, group):
                    arrived(other(d), 2 + 2 * j)

    for copy in block_copies(0, q, True, g, 0):
        copy.wait_send()
    for j in (1, 0, 2):
        for up, computes, sends in cases(j):
            @pl.when(sends)
            def _():
                margin_copy(j, up).wait_send()

            @pl.when(computes)
            def _():
                for target in pair_targets(j, up):
                    for copy in block_copies(*target):
                        copy.wait_send()


def local(lines, group, margin_basis, pair_matrix, own_basis, own_image, tile_counts):
    _, _, rows, eig = margin_basis.shape
    own_rows = own_basis.shape[1]
    share = eig // group
    blocks = pl.pallas_call(
        functools.partial(kernel, lines, group),
        out_shape=jax.ShapeDtypeStruct((group, 7, share, eig), BF16),
        in_specs=[pl.BlockSpec(memory_space=pltpu.SMEM)] + [pl.BlockSpec(memory_space=pltpu.HBM)] * 4,
        out_specs=pl.BlockSpec(memory_space=pltpu.VMEM),
        scratch_shapes=[
            pltpu.VMEM((3, rows, eig), BF16),
            pltpu.VMEM((3, rows, eig), BF16),
            pltpu.VMEM((3, rows, rows), BF16),
            pltpu.VMEM((own_rows, eig), BF16),
            pltpu.VMEM((own_rows, eig), BF16),
            pltpu.VMEM((3, rows, eig), BF16),
            pltpu.VMEM((7, group, share, eig), BF16),
            pltpu.SemaphoreType.DMA((8,)),
            pltpu.SemaphoreType.DMA((3,)),
            pltpu.SemaphoreType.DMA((3,)),
            pltpu.SemaphoreType.DMA((7, group)),
            pltpu.SemaphoreType.DMA((group, 7)),
        ],
        compiler_params=pltpu.CompilerParams(
            collective_id=0, has_side_effects=True, vmem_limit_bytes=24 * 1024 * 1024
        ),
    )(tile_counts, margin_basis, pair_matrix, own_basis, own_image)
    return blocks.astype(F32)


def solution(mesh):
    return jax.shard_map(
        functools.partial(local, mesh.shape["sub"], mesh.shape["grp"]),
        mesh=mesh,
        in_specs=(
            P(("sub", "grp"), None, None, None),
            P(("sub", "grp"), None, None, None),
            P(("sub", "grp"), None, None),
            P(("sub", "grp"), None, None),
            P(("sub", "grp"), None),
        ),
        out_specs=P("sub", None, "grp", None),
        check_vma=False,
    )
```

```python
import functools

import jax
import jax.numpy as jnp
from jax import lax
from jax.experimental import pallas as pl
from jax.experimental.pallas import tpu as pltpu
from jax.sharding import PartitionSpec as P

ROW_TILE = 128
SPAN = 8
MESH = pl.DeviceIdType.MESH
F32 = jnp.float32
BF16 = jnp.bfloat16


def contract_rows(left, right):
    return lax.dot_general(left, right, (((0,), (0,)), ((), ())), preferred_element_type=F32)


def masked(block, tile_count):
    row_index = lax.broadcasted_iota(jnp.int32, block.shape, 0)
    return jnp.where(row_index < tile_count * ROW_TILE, block, jnp.zeros((), block.dtype))


def kernel(
    lines, group,
    counts, margin, matrix, own_basis, own_image, out,
    m_own, m_got, mats, basis, image, applied, stage,
    load_sem, margin_send, margin_recv, block_send, block_recv,
):
    q = lax.axis_index("sub")
    g = lax.axis_index("grp")
    odd = lax.rem(q, 2) == 1

    directions = (
        (odd, g >= 1, g + 1 < group, (0, 1)),
        (True, q >= 1, q + 1 < lines, (1, 0)),
        (odd, q >= SPAN, q + SPAN < lines, (SPAN, 0)),
    )

    def cases(j):
        up, low, high, _ = directions[j]
        if up is True:
            return ((True, low, high),)
        return (
            (True, jnp.logical_and(up, low), jnp.logical_and(up, high)),
            (False, jnp.logical_and(jnp.logical_not(up), high), jnp.logical_and(jnp.logical_not(up), low)),
        )

    def other(d):
        return lax.rem(g + d, group)

    barrier = pltpu.get_barrier_semaphore()
    for d in range(1, group):
        pl.semaphore_signal(barrier, inc=1, device_id=(q, other(d)), device_id_type=MESH)
    greeted = jnp.int32(group - 1)
    for j in (1, 2):
        _, low, high, (step, _) = directions[j]
        for there, line in ((low, q - step), (high, q + step)):
            @pl.when(there)
            def _():
                for d in range(group):
                    pl.semaphore_signal(barrier, inc=1, device_id=(line, other(d)), device_id_type=MESH)
            greeted = greeted + jnp.where(there, group, 0)

    load_basis = pltpu.make_async_copy(own_basis.at[0], basis, load_sem.at[6])
    load_image = pltpu.make_async_copy(own_image.at[0], image, load_sem.at[7])

    def loads(j, up):
        slot = 2 * j + (1 if up else 0)
        return (
            pltpu.make_async_copy(margin.at[0, slot], m_own.at[j], load_sem.at[2 * j]),
            pltpu.make_async_copy(matrix.at[0, slot], mats.at[j], load_sem.at[2 * j + 1]),
        )

    load_basis.start()
    load_image.start()
    for j in (1, 0, 2):
        for up, computes, _ in cases(j):
            @pl.when(computes)
            def _():
                for copy in loads(j, up):
                    copy.start()

    def margin_copy(j, up):
        sq, sg = directions[j][3]
        target = (q + sq, g + sg) if up else (q - sq, g - sg)
        slot = 2 * j + (0 if up else 1)
        return pltpu.make_async_remote_copy(
            src_ref=margin.at[0, slot], dst_ref=m_got.at[j],
            send_sem=margin_send.at[j], recv_sem=margin_recv.at[j],
            device_id=target, device_id_type=MESH,
        )

    pl.semaphore_wait(barrier, greeted)
    for j in (2, 1, 0):
        for up, _, sends in cases(j):
            @pl.when(sends)
            def _():
                margin_copy(j, up).start()

    def block_copies(block, line, own_line, place, slot):
        return [
            pltpu.make_async_remote_copy(
                src_ref=stage.at[block, other(d)], dst_ref=out.at[place, slot],
                send_sem=block_send.at[block, d], recv_sem=block_recv.at[place, slot],
                device_id=(line, other(d)), device_id_type=MESH,
            )
            for d in range(1 if own_line else 0, group)
        ]

    def deliver(block, value, line, own_line, place, slot):
        stage[block] = value.astype(BF16).reshape(stage.shape[1:])
        for copy in block_copies(block, line, own_line, place, slot):
            copy.start()
        if own_line:
            out[place, slot] = stage[block, g]

    def pair_targets(j, up):
        sq, sg = directions[j][3]
        lower = (q - sq, g - sg) if up else (q, g)
        upper = (q, g) if up else (q + sq, g + sg)
        own_lower = sq == 0 or not up
        own_upper = sq == 0 or up
        return (
            (1 + 2 * j, lower[0], own_lower, lower[1], 1 + 2 * j),
            (2 + 2 * j, upper[0], own_upper, upper[1], 2 + 2 * j),
        )

    load_basis.wait()
    load_image.wait()
    deliver(0, contract_rows(basis[...], image[...]), q, True, g, 0)

    nothing = jnp.zeros(out.shape[2:], BF16)
    out[group - 1, 1] = nothing
    out[0, 2] = nothing
    for j in (1, 2):
        _, low, high, _ = directions[j]
        for there, slot in ((high, 1 + 2 * j), (low, 2 + 2 * j)):
            @pl.when(jnp.logical_not(there))
            def _():
                for place in range(group):
                    out[place, slot] = nothing

    for j in (1, 0, 2):
        for up, computes, _ in cases(j):
            @pl.when(computes)
            def _():
                for copy in loads(j, up):
                    copy.wait()
                if up:
                    count = counts[0, 2 * j + 1]
                    product = contract_rows(mats[j], masked(m_own[j], count))
                    applied[j] = masked(product, count).astype(BF16)

    for j in (1, 0, 2):
        for up, computes, _ in cases(j):
            @pl.when(computes)
            def _():
                margin_copy(j, up).wait_recv()
                if up:
                    coupling = contract_rows(m_got[j], applied[j])
                else:
                    count = counts[0, 2 * j]
                    product = jnp.dot(mats[j], masked(m_got[j], count), preferred_element_type=F32)
                    coupling = contract_rows(m_own[j], masked(product, count).astype(BF16))
                first, second = pair_targets(j, up)
                deliver(first[0], coupling, *first[1:])
                deliver(second[0], coupling.T, *second[1:])

    def arrived(place, slot):
        pltpu.make_async_remote_copy(
            src_ref=stage.at[0, 0], dst_ref=out.at[place, slot],
            send_sem=block_send.at[0, 0], recv_sem=block_recv.at[place, slot],
            device_id=(q, other(1)), device_id_type=MESH,
        ).wait_recv()

    for d in range(1, group):
        arrived(other(d), 0)
    for place in range(group - 1):
        @pl.when(jnp.where(odd, place + 1, place) != g)
        def _():
            arrived(place, 1)
            arrived(place + 1, 2)
    for j in (1, 2):
        up, low, high, _ = directions[j]
        for at_upper in (True, False):
            if up is True:
                if not at_upper:
                    continue
                high_here, low_here = high, low
            else:
                chosen = up if at_upper else jnp.logical_not(up)
                high_here, low_here = jnp.logical_and(chosen, high), jnp.logical_and(chosen, low)

            @pl.when(high_here)
            def _():
                for d in range(0 if at_upper else 1, group):
                    arrived(other(d), 1 + 2 * j)

            @pl.when(low_here)
            def _():
                for d in range(1 if at_upper else 0, group):
                    arrived(other(d), 2 + 2 * j)

    for copy in block_copies(0, q, True, g, 0):
        copy.wait_send()
    for j in (1, 0, 2):
        for up, computes, sends in cases(j):
            @pl.when(sends)
            def _():
                margin_copy(j, up).wait_send()

            @pl.when(computes)
            def _():
                for target in pair_targets(j, up):
                    for copy in block_copies(*target):
                        copy.wait_send()


def local(lines, group, margin_basis, pair_matrix, own_basis, own_image, tile_counts):
    _, _, rows, eig = margin_basis.shape
    own_rows = own_basis.shape[1]
    share = eig // group
    blocks = pl.pallas_call(
        functools.partial(kernel, lines, group),
        out_shape=pltpu.VMEM((group, 7, share, eig), BF16),
        in_specs=[pl.BlockSpec(memory_space=pltpu.SMEM)] + [pl.BlockSpec(memory_space=pltpu.HBM)] * 4,
        out_specs=pl.BlockSpec(memory_space=pltpu.VMEM),
        scratch_shapes=[
            pltpu.VMEM((3, rows, eig), BF16),
            pltpu.VMEM((3, rows, eig), BF16),
            pltpu.VMEM((3, rows, rows), BF16),
            pltpu.VMEM((own_rows, eig), BF16),
            pltpu.VMEM((own_rows, eig), BF16),
            pltpu.VMEM((3, rows, eig), BF16),
            pltpu.VMEM((7, group, share, eig), BF16),
            pltpu.SemaphoreType.DMA((8,)),
            pltpu.SemaphoreType.DMA((3,)),
            pltpu.SemaphoreType.DMA((3,)),
            pltpu.SemaphoreType.DMA((7, group)),
            pltpu.SemaphoreType.DMA((group, 7)),
        ],
        compiler_params=pltpu.CompilerParams(
            collective_id=0, has_side_effects=True
        ),
    )(tile_counts, margin_basis, pair_matrix, own_basis, own_image)
    return blocks.astype(F32)


def solution(mesh):
    return jax.shard_map(
        functools.partial(local, mesh.shape["sub"], mesh.shape["grp"]),
        mesh=mesh,
        in_specs=(
            P(("sub", "grp"), None, None, None),
            P(("sub", "grp"), None, None, None),
            P(("sub", "grp"), None, None),
            P(("sub", "grp"), None, None),
            P(("sub", "grp"), None),
        ),
        out_specs=P("sub", None, "grp", None),
        check_vma=False,
    )
```

```python
import functools

import jax
import jax.numpy as jnp
from jax import lax
from jax.experimental import pallas as pl
from jax.experimental.pallas import tpu as pltpu
from jax.sharding import PartitionSpec as P

ROW_TILE = 128
SPAN = 8
MESH = pl.DeviceIdType.MESH
F32 = jnp.float32
BF16 = jnp.bfloat16


def contract_rows(left, right):
    return lax.dot_general(left, right, (((0,), (0,)), ((), ())), preferred_element_type=F32)


def masked(block, tile_count):
    row_index = lax.broadcasted_iota(jnp.int32, block.shape, 0)
    return jnp.where(row_index < tile_count * ROW_TILE, block, jnp.zeros((), block.dtype))


def kernel(
    lines, group,
    counts, margin, matrix, own_basis, own_image, out,
    m_own, m_got, mats, basis, image, applied, stage,
    load_sem, margin_send, margin_recv, block_send, block_recv,
):
    q = lax.axis_index("sub")
    g = lax.axis_index("grp")
    odd = lax.rem(q, 2) == 1

    directions = (
        (odd, g >= 1, g + 1 < group, (0, 1)),
        (True, q >= 1, q + 1 < lines, (1, 0)),
        (odd, q >= SPAN, q + SPAN < lines, (SPAN, 0)),
    )

    def cases(j):
        up, low, high, _ = directions[j]
        if up is True:
            return ((True, low, high),)
        return (
            (True, jnp.logical_and(up, low), jnp.logical_and(up, high)),
            (False, jnp.logical_and(jnp.logical_not(up), high), jnp.logical_and(jnp.logical_not(up), low)),
        )

    def other(d):
        return lax.rem(g + d, group)

    barrier = pltpu.get_barrier_semaphore()
    greeted = jnp.int32(group - 1)
    for j in (2, 1):
        step = directions[j][3][0]
        for up, computes, sends in cases(j):
            @pl.when(computes)
            def _():
                source = (q - step, g) if up else (q + step, g)
                pl.semaphore_signal(barrier, inc=1, device_id=source, device_id_type=MESH)
            greeted = greeted + jnp.where(sends, 1, 0)
    for d in range(1, group):
        pl.semaphore_signal(barrier, inc=1, device_id=(q, other(d)), device_id_type=MESH)

    load_basis = pltpu.make_async_copy(own_basis.at[0], basis, load_sem.at[6])
    load_image = pltpu.make_async_copy(own_image.at[0], image, load_sem.at[7])

    def loads(j, up):
        slot = 2 * j + (1 if up else 0)
        return (
            pltpu.make_async_copy(margin.at[0, slot], m_own.at[j], load_sem.at[2 * j]),
            pltpu.make_async_copy(matrix.at[0, slot], mats.at[j], load_sem.at[2 * j + 1]),
        )

    load_basis.start()
    load_image.start()
    for j in (1, 0, 2):
        for up, computes, _ in cases(j):
            @pl.when(computes)
            def _():
                for copy in loads(j, up):
                    copy.start()

    def margin_copy(j, up):
        sq, sg = directions[j][3]
        target = (q + sq, g + sg) if up else (q - sq, g - sg)
        slot = 2 * j + (0 if up else 1)
        return pltpu.make_async_remote_copy(
            src_ref=margin.at[0, slot], dst_ref=m_got.at[j],
            send_sem=margin_send.at[j], recv_sem=margin_recv.at[j],
            device_id=target, device_id_type=MESH,
        )

    pl.semaphore_wait(barrier, greeted)
    for j in (1, 2, 0):
        for up, _, sends in cases(j):
            @pl.when(sends)
            def _():
                margin_copy(j, up).start()

    def block_copies(block, line, own_line, place, slot):
        return [
            pltpu.make_async_remote_copy(
                src_ref=stage.at[block, other(d)], dst_ref=out.at[place, slot],
                send_sem=block_send.at[block, d], recv_sem=block_recv.at[place, slot],
                device_id=(line, other(d)), device_id_type=MESH,
            )
            for d in reversed(range(1 if own_line else 0, group))
        ]

    def deliver(block, value, line, own_line, place, slot):
        stage[block] = value.astype(BF16).reshape(stage.shape[1:])
        for copy in block_copies(block, line, own_line, place, slot):
            copy.start()
        if own_line:
            out[place, slot] = stage[block, g]

    def pair_targets(j, up):
        sq, sg = directions[j][3]
        lower = (q - sq, g - sg) if up else (q, g)
        upper = (q, g) if up else (q + sq, g + sg)
        own_lower = sq == 0 or not up
        own_upper = sq == 0 or up
        return (
            (1 + 2 * j, lower[0], own_lower, lower[1], 1 + 2 * j),
            (2 + 2 * j, upper[0], own_upper, upper[1], 2 + 2 * j),
        )

    load_basis.wait()
    load_image.wait()
    deliver(0, contract_rows(basis[...], image[...]), q, True, g, 0)

    nothing = jnp.zeros(out.shape[2:], BF16)
    out[group - 1, 1] = nothing
    out[0, 2] = nothing
    for j in (1, 2):
        _, low, high, _ = directions[j]
        for there, slot in ((high, 1 + 2 * j), (low, 2 + 2 * j)):
            @pl.when(jnp.logical_not(there))
            def _():
                for place in range(group):
                    out[place, slot] = nothing

    for j in (1, 0, 2):
        for up, computes, _ in cases(j):
            @pl.when(computes)
            def _():
                for copy in loads(j, up):
                    copy.wait()
                if up:
                    count = counts[0, 2 * j + 1]
                    product = contract_rows(mats[j], masked(m_own[j], count))
                    applied[j] = masked(product, count).astype(BF16)

    for j in (1, 0, 2):
        for up, computes, _ in cases(j):
            @pl.when(computes)
            def _():
                margin_copy(j, up).wait_recv()
                if up:
                    coupling = contract_rows(m_got[j], applied[j])
                else:
                    count = counts[0, 2 * j]
                    product = jnp.dot(mats[j], masked(m_got[j], count), preferred_element_type=F32)
                    coupling = contract_rows(m_own[j], masked(product, count).astype(BF16))
                first, second = pair_targets(j, up)
                if up:
                    deliver(first[0], coupling, *first[1:])
                    deliver(second[0], coupling.T, *second[1:])
                else:
                    deliver(second[0], coupling.T, *second[1:])
                    deliver(first[0], coupling, *first[1:])

    def arrived(place, slot):
        pltpu.make_async_remote_copy(
            src_ref=stage.at[0, 0], dst_ref=out.at[place, slot],
            send_sem=block_send.at[0, 0], recv_sem=block_recv.at[place, slot],
            device_id=(q, other(1)), device_id_type=MESH,
        ).wait_recv()

    for d in range(1, group):
        arrived(other(d), 0)
    for place in range(group - 1):
        @pl.when(jnp.where(odd, place + 1, place) != g)
        def _():
            arrived(place, 1)
            arrived(place + 1, 2)
    for j in (1, 2):
        up, low, high, _ = directions[j]
        for at_upper in (True, False):
            if up is True:
                if not at_upper:
                    continue
                high_here, low_here = high, low
            else:
                chosen = up if at_upper else jnp.logical_not(up)
                high_here, low_here = jnp.logical_and(chosen, high), jnp.logical_and(chosen, low)

            @pl.when(high_here)
            def _():
                for d in range(0 if at_upper else 1, group):
                    arrived(other(d), 1 + 2 * j)

            @pl.when(low_here)
            def _():
                for d in range(1 if at_upper else 0, group):
                    arrived(other(d), 2 + 2 * j)

    for copy in block_copies(0, q, True, g, 0):
        copy.wait_send()
    for j in (1, 0, 2):
        for up, computes, sends in cases(j):
            @pl.when(sends)
            def _():
                margin_copy(j, up).wait_send()

            @pl.when(computes)
            def _():
                for target in pair_targets(j, up):
                    for copy in block_copies(*target):
                        copy.wait_send()


def local(lines, group, margin_basis, pair_matrix, own_basis, own_image, tile_counts):
    _, _, rows, eig = margin_basis.shape
    own_rows = own_basis.shape[1]
    share = eig // group
    blocks = pl.pallas_call(
        functools.partial(kernel, lines, group),
        out_shape=pltpu.VMEM((group, 7, share, eig), BF16),
        in_specs=[pl.BlockSpec(memory_space=pltpu.SMEM)] + [pl.BlockSpec(memory_space=pltpu.HBM)] * 4,
        out_specs=pl.BlockSpec(memory_space=pltpu.VMEM),
        scratch_shapes=[
            pltpu.VMEM((3, rows, eig), BF16),
            pltpu.VMEM((3, rows, eig), BF16),
            pltpu.VMEM((3, rows, rows), BF16),
            pltpu.VMEM((own_rows, eig), BF16),
            pltpu.VMEM((own_rows, eig), BF16),
            pltpu.VMEM((3, rows, eig), BF16),
            pltpu.VMEM((7, group, share, eig), BF16),
            pltpu.SemaphoreType.DMA((8,)),
            pltpu.SemaphoreType.DMA((3,)),
            pltpu.SemaphoreType.DMA((3,)),
            pltpu.SemaphoreType.DMA((7, group)),
            pltpu.SemaphoreType.DMA((group, 7)),
        ],
        compiler_params=pltpu.CompilerParams(
            collective_id=0, has_side_effects=True
        ),
    )(tile_counts, margin_basis, pair_matrix, own_basis, own_image)
    return blocks.astype(F32)


def solution(mesh):
    return jax.shard_map(
        functools.partial(local, mesh.shape["sub"], mesh.shape["grp"]),
        mesh=mesh,
        in_specs=(
            P(("sub", "grp"), None, None, None),
            P(("sub", "grp"), None, None, None),
            P(("sub", "grp"), None, None),
            P(("sub", "grp"), None, None),
            P(("sub", "grp"), None),
        ),
        out_specs=P("sub", None, "grp", None),
        check_vma=False,
    )
```

```python
import functools

import jax
import jax.numpy as jnp
from jax import lax
from jax.experimental import pallas as pl
from jax.experimental.pallas import tpu as pltpu
from jax.sharding import PartitionSpec as P

ROW_TILE = 128
SPAN = 8
MESH = pl.DeviceIdType.MESH
F32 = jnp.float32
BF16 = jnp.bfloat16


def contract_rows(left, right):
    return lax.dot_general(left, right, (((0,), (0,)), ((), ())), preferred_element_type=F32)


def masked(block, tile_count):
    row_index = lax.broadcasted_iota(jnp.int32, block.shape, 0)
    return jnp.where(row_index < tile_count * ROW_TILE, block, jnp.zeros((), block.dtype))


def kernel(
    lines, group,
    counts, margin, matrix, own_basis, own_image, out,
    m_own, m_sent, m_got, mats, basis, image, applied, rest, stage,
    load_sem, margin_send, margin_recv, block_send, block_recv,
):
    q = lax.axis_index("sub")
    g = lax.axis_index("grp")
    odd = lax.rem(q, 2) == 1

    directions = (
        (odd, g >= 1, g + 1 < group, (0, 1)),
        (True, q >= 1, q + 1 < lines, (1, 0)),
        (odd, q >= SPAN, q + SPAN < lines, (SPAN, 0)),
    )

    def cases(j):
        up, low, high, _ = directions[j]
        if up is True:
            return ((True, low, high),)
        return (
            (True, jnp.logical_and(up, low), jnp.logical_and(up, high)),
            (False, jnp.logical_and(jnp.logical_not(up), high), jnp.logical_and(jnp.logical_not(up), low)),
        )

    def other(d):
        return lax.rem(g + d, group)

    barrier = pltpu.get_barrier_semaphore()
    greeted = jnp.int32(group - 1)
    for j in (2, 1):
        step = directions[j][3][0]
        for up, computes, sends in cases(j):
            @pl.when(computes)
            def _():
                source = (q - step, g) if up else (q + step, g)
                pl.semaphore_signal(barrier, inc=1, device_id=source, device_id_type=MESH)
            greeted = greeted + jnp.where(sends, 1, 0)
    for d in range(1, group):
        pl.semaphore_signal(barrier, inc=1, device_id=(q, other(d)), device_id_type=MESH)

    load_basis = pltpu.make_async_copy(own_basis.at[0], basis, load_sem.at[6])
    load_image = pltpu.make_async_copy(own_image.at[0], image, load_sem.at[7])

    def sent_load(j, up):
        return pltpu.make_async_copy(margin.at[0, 2 * j + (0 if up else 1)], m_sent.at[j], load_sem.at[8 + j])

    def loads(j, up):
        slot = 2 * j + (1 if up else 0)
        return (
            pltpu.make_async_copy(margin.at[0, slot], m_own.at[j], load_sem.at[2 * j]),
            pltpu.make_async_copy(matrix.at[0, slot], mats.at[j], load_sem.at[2 * j + 1]),
        )

    for j in (1, 2, 0):
        for up, _, sends in cases(j):
            @pl.when(sends)
            def _():
                sent_load(j, up).start()
    load_basis.start()
    load_image.start()
    for j in (1, 0, 2):
        for up, computes, _ in cases(j):
            @pl.when(computes)
            def _():
                for copy in loads(j, up):
                    copy.start()

    def margin_copy(j, up):
        sq, sg = directions[j][3]
        target = (q + sq, g + sg) if up else (q - sq, g - sg)
        slot = 2 * j + (0 if up else 1)
        return pltpu.make_async_remote_copy(
            src_ref=m_sent.at[j], dst_ref=m_got.at[j],
            send_sem=margin_send.at[j], recv_sem=margin_recv.at[j],
            device_id=target, device_id_type=MESH,
        )

    pl.semaphore_wait(barrier, greeted)
    for j in (1, 2, 0):
        for up, _, sends in cases(j):
            @pl.when(sends)
            def _():
                sent_load(j, up).wait()
                margin_copy(j, up).start()

    def block_copies(block, line, own_line, place, slot):
        return [
            pltpu.make_async_remote_copy(
                src_ref=stage.at[block, other(d)], dst_ref=out.at[place, slot],
                send_sem=block_send.at[block, d], recv_sem=block_recv.at[place, slot],
                device_id=(line, other(d)), device_id_type=MESH,
            )
            for d in reversed(range(1 if own_line else 0, group))
        ]

    def deliver(block, value, line, own_line, place, slot):
        stage[block] = value.astype(BF16).reshape(stage.shape[1:])
        for copy in block_copies(block, line, own_line, place, slot):
            copy.start()
        if own_line:
            out[place, slot] = stage[block, g]

    def pair_targets(j, up):
        sq, sg = directions[j][3]
        lower = (q - sq, g - sg) if up else (q, g)
        upper = (q, g) if up else (q + sq, g + sg)
        own_lower = sq == 0 or not up
        own_upper = sq == 0 or up
        return (
            (1 + 2 * j, lower[0], own_lower, lower[1], 1 + 2 * j),
            (2 + 2 * j, upper[0], own_upper, upper[1], 2 + 2 * j),
        )

    load_basis.wait()
    load_image.wait()
    deliver(0, contract_rows(basis[...], image[...]), q, True, g, 0)

    nothing = jnp.zeros(out.shape[2:], BF16)
    out[group - 1, 1] = nothing
    out[0, 2] = nothing
    for j in (1, 2):
        _, low, high, _ = directions[j]
        for there, slot in ((high, 1 + 2 * j), (low, 2 + 2 * j)):
            @pl.when(jnp.logical_not(there))
            def _():
                for place in range(group):
                    out[place, slot] = nothing

    for j in (1, 0, 2):
        for up, computes, _ in cases(j):
            @pl.when(computes)
            def _():
                for copy in loads(j, up):
                    copy.wait()
                if up:
                    count = counts[0, 2 * j + 1]
                    product = contract_rows(mats[j], masked(m_own[j], count))
                    applied[j] = masked(product, count).astype(BF16)
                else:
                    count = counts[0, 2 * j]
                    product = masked(contract_rows(mats[j], masked(m_own[j], count)), count)
                    applied[j] = product.astype(BF16)
                    rest[j] = (product - applied[j].astype(F32)).astype(BF16)

    for j in (1, 0, 2):
        for up, computes, _ in cases(j):
            @pl.when(computes)
            def _():
                margin_copy(j, up).wait_recv()
                if up:
                    coupling = contract_rows(m_got[j], applied[j])
                else:
                    coupling = contract_rows(applied[j], m_got[j]) + contract_rows(rest[j], m_got[j])
                first, second = pair_targets(j, up)
                if up:
                    deliver(first[0], coupling, *first[1:])
                    deliver(second[0], coupling.T, *second[1:])
                else:
                    deliver(second[0], coupling.T, *second[1:])
                    deliver(first[0], coupling, *first[1:])

    def arrived(place, slot):
        pltpu.make_async_remote_copy(
            src_ref=stage.at[0, 0], dst_ref=out.at[place, slot],
            send_sem=block_send.at[0, 0], recv_sem=block_recv.at[place, slot],
            device_id=(q, other(1)), device_id_type=MESH,
        ).wait_recv()

    for d in range(1, group):
        arrived(other(d), 0)
    for place in range(group - 1):
        @pl.when(jnp.where(odd, place + 1, place) != g)
        def _():
            arrived(place, 1)
            arrived(place + 1, 2)
    for j in (1, 2):
        up, low, high, _ = directions[j]
        for at_upper in (True, False):
            if up is True:
                if not at_upper:
                    continue
                high_here, low_here = high, low
            else:
                chosen = up if at_upper else jnp.logical_not(up)
                high_here, low_here = jnp.logical_and(chosen, high), jnp.logical_and(chosen, low)

            @pl.when(high_here)
            def _():
                for d in range(0 if at_upper else 1, group):
                    arrived(other(d), 1 + 2 * j)

            @pl.when(low_here)
            def _():
                for d in range(1 if at_upper else 0, group):
                    arrived(other(d), 2 + 2 * j)

    for copy in block_copies(0, q, True, g, 0):
        copy.wait_send()
    for j in (1, 0, 2):
        for up, computes, sends in cases(j):
            @pl.when(sends)
            def _():
                margin_copy(j, up).wait_send()

            @pl.when(computes)
            def _():
                for target in pair_targets(j, up):
                    for copy in block_copies(*target):
                        copy.wait_send()


def local(lines, group, margin_basis, pair_matrix, own_basis, own_image, tile_counts):
    _, _, rows, eig = margin_basis.shape
    own_rows = own_basis.shape[1]
    share = eig // group
    blocks = pl.pallas_call(
        functools.partial(kernel, lines, group),
        out_shape=pltpu.VMEM((group, 7, share, eig), BF16),
        in_specs=[pl.BlockSpec(memory_space=pltpu.SMEM)] + [pl.BlockSpec(memory_space=pltpu.HBM)] * 4,
        out_specs=pl.BlockSpec(memory_space=pltpu.VMEM),
        scratch_shapes=[
            pltpu.VMEM((3, rows, eig), BF16),
            pltpu.VMEM((3, rows, eig), BF16),
            pltpu.VMEM((3, rows, eig), BF16),
            pltpu.VMEM((3, rows, rows), BF16),
            pltpu.VMEM((own_rows, eig), BF16),
            pltpu.VMEM((own_rows, eig), BF16),
            pltpu.VMEM((3, rows, eig), BF16),
            pltpu.VMEM((3, rows, eig), BF16),
            pltpu.VMEM((7, group, share, eig), BF16),
            pltpu.SemaphoreType.DMA((11,)),
            pltpu.SemaphoreType.DMA((3,)),
            pltpu.SemaphoreType.DMA((3,)),
            pltpu.SemaphoreType.DMA((7, group)),
            pltpu.SemaphoreType.DMA((group, 7)),
        ],
        compiler_params=pltpu.CompilerParams(
            collective_id=0, has_side_effects=True
        ),
    )(tile_counts, margin_basis, pair_matrix, own_basis, own_image)
    return blocks.astype(F32)


def solution(mesh):
    return jax.shard_map(
        functools.partial(local, mesh.shape["sub"], mesh.shape["grp"]),
        mesh=mesh,
        in_specs=(
            P(("sub", "grp"), None, None, None),
            P(("sub", "grp"), None, None, None),
            P(("sub", "grp"), None, None),
            P(("sub", "grp"), None, None),
            P(("sub", "grp"), None),
        ),
        out_specs=P("sub", None, "grp", None),
        check_vma=False,
    )
```
